512 devices in a mesh: img: 64 (over x, y, z_lo), bas: 8 (over z_hi, core).
Axes of the slice: x: 4, y: 4, z: 16 (z_hi: 4, z_lo: 4; z = z_hi * 4 + z_lo), core: 2. Of those that a mesh axis runs over, the one named last changes fastest.
Arguments:
- polar_images: bfloat16 [2048, 64, 512], P('img', 'bas'), may hold values from -6 to 6
- ctf_groups: int32 [2048], P('img'), may hold values from 0 to 63
- ctf_table: float32 [64, 64], replicated, may hold values from -1 to 1
- radial_basis: bfloat16 [256, 64, 64], P('bas'), may hold values from -0.75 to 0.75
- order_counts: int32 [256], P('bas'), may hold values from 1 to 64, as said below
Outputs:
- covariance: float32 [64, 16384], P('img', 'bas')
The draws below stay inside these ranges and needn't reach their ends.
Inputs may be any that keep to these rules, and one draw needn't show every extreme that they name: `order_counts`: order 0 has 64 basis functions; every other order q has max(1, 64 - (q * 64) // 256 - j) of them, where j is one of 0, 1, 2, 3 and may differ from order to order.
All inputs are finite; a program needn't handle non-finite values.
Results may differ from the reference program's by a relative error of at most 0.0015.
Values may be sent and summed in bfloat16 or wider, within the bound.
No kernel may reach another device: no remote copies, remote signals or barrier semaphores. Data moves between devices by JAX's collectives and lax.ppermute only.
A program may use at most 64 MiB of HBM per device.

```python
import math
import jax
import jax.numpy as jnp
from jax import lax

NQ = 256
NR = 64
NA = 512
KMAX = 64
GROUPS = 64
IMG_DEV = 32
IMAGES = 2048
N_IMG = 64


def draw_order_counts(key, part):
    key = jax.random.fold_in(key, 11)
    orders = jnp.arange(NQ, dtype=jnp.int32)
    base = KMAX - orders * KMAX // NQ
    jitter = jax.random.randint(key, (NQ,), 0, 4, dtype=jnp.int32)
    counts = jnp.clip(base - jitter, 1, KMAX)
    counts = jnp.where(orders == 0, KMAX, counts)
    return counts.astype(jnp.int32)


def plant(result, stream_key, smallest, top_value):
    extent = result.shape
    index_at = [jax.random.randint(jax.random.fold_in(stream_key, axis), (), 0, extent[axis]) for axis in range(len(extent))]
    result = result.at[tuple(index_at)].set(smallest)
    longest = extent.index(max(extent))
    index_at[longest] = (index_at[longest] + 1) % extent[longest]
    return result.at[tuple(index_at)].set(top_value)


def level_of(own_key, shape, cuts, least, high):
    def one(axis_at, parts):
        steps = jax.random.uniform(jax.random.fold_in(jax.random.fold_in(own_key, 6), axis_at), (parts,), jnp.float32, least / len(cuts), high / len(cuts))
        return jnp.repeat(jnp.exp(steps), shape[axis_at] // parts).reshape((-1,) + (1,) * (len(shape) - axis_at - 1))

    factor_of = one(*cuts[0])
    for cut in cuts[1:]:
        factor_of = factor_of * one(*cut)
    return factor_of


def scatter_about(own_key, dims, scale, most, shards=(), kind=jnp.bfloat16):
    array = jax.random.normal(own_key, dims, jnp.float32) * scale
    if len(shards) > 0:
        array = level_of(own_key, dims, shards, -0.22, 0.18) * array
    return jnp.clip(array, min=-most, max=most).astype(kind)


def setup_inputs(seed: int = 0) -> dict:
    key_of = jax.random.split(jax.random.key(seed), 6)
    polar_images = scatter_about(key_of[0], (IMAGES, NR, NA), 1.0, 6.0, ((0, 64), (1, 8)))
    ctf_groups = plant(jax.random.randint(key_of[1], (IMAGES,), 0, GROUPS), jax.random.fold_in(key_of[1], 1), 0, GROUPS - 1).astype(jnp.int32)
    ctf_table = jnp.clip(jax.random.uniform(key_of[2], (GROUPS, NR), jnp.float32, -1.0, 1.0), -1.0, 1.0)
    radial_basis = scatter_about(key_of[3], (NQ, NR, KMAX), NR ** -0.5, 0.75, ((0, 8),))
    order_counts = draw_order_counts(jax.random.fold_in(key_of[5], 71), 0)
    return dict(polar_images=polar_images, ctf_groups=ctf_groups, ctf_table=ctf_table, radial_basis=radial_basis, order_counts=order_counts)


def angular_table(orders, angles):
    steps = jnp.arange(angles, dtype=jnp.int32)
    phase = steps[:, None] * orders[None, :] % angles
    theta = phase.astype(jnp.float32) * (2.0 * math.pi / angles)
    table = jnp.stack([jnp.cos(theta), jnp.sin(theta)], axis=-1) * (1.0 / math.sqrt(angles))
    return table.reshape(angles, -1).astype(jnp.bfloat16)

def reference(polar_images, ctf_groups, ctf_table, radial_basis, order_counts):
    table = angular_table(jnp.arange(NQ, dtype=jnp.int32), NA)
    kept = (jnp.arange(KMAX, dtype=jnp.int32)[None, :] < order_counts[:, None]).astype(jnp.float32)
    basis_wide = radial_basis.astype(jnp.float32)
    blocks = polar_images.reshape(N_IMG, IMG_DEV, NR, NA)
    labels = ctf_groups.reshape(N_IMG, IMG_DEV)

    def accumulate(gram, block):
        images, groups = block
        weights = ctf_table[groups]
        weighted = (images.astype(jnp.float32) * weights[:, :, None]).astype(jnp.bfloat16)
        spectra = jnp.dot(weighted.reshape(-1, NA), table, preferred_element_type=jnp.float32)
        spectra = lax.optimization_barrier(spectra.astype(jnp.bfloat16))
        spectra = spectra.astype(jnp.float32).reshape(IMG_DEV, NR, NQ, 2)
        coeffs = jnp.einsum('brqc,qrk->bqck', spectra, basis_wide)
        coeffs = lax.optimization_barrier((coeffs * kept[None, :, None, :]).astype(jnp.bfloat16))
        coeffs = coeffs.astype(jnp.float32)
        return (gram + jnp.einsum('bqck,bqcl->kql', coeffs, coeffs), None)
    gram, _ = lax.scan(accumulate, jnp.zeros((KMAX, NQ, KMAX), jnp.float32), (blocks, labels))
    return (gram / IMAGES).reshape(KMAX, NQ * KMAX)
```

```python
import math

import jax
import jax.numpy as jnp
from jax import lax
from jax.sharding import PartitionSpec as P


def angular_table(orders, angles):
    steps = jnp.arange(angles, dtype=jnp.int32)
    phase = steps[:, None] * orders[None, :] % angles
    theta = phase.astype(jnp.float32) * (2.0 * math.pi / angles)
    table = jnp.stack([jnp.cos(theta), jnp.sin(theta)], axis=-1) * (1.0 / math.sqrt(angles))
    return table.reshape(angles, -1).astype(jnp.bfloat16)


def local(polar_images, ctf_groups, ctf_table, radial_basis, order_counts):
    images_dev, radii_dev, angles = polar_images.shape
    orders_dev, radii, kmax = radial_basis.shape
    img_size, bas_size = lax.axis_size("img"), lax.axis_size("bas")
    classes = ctf_table.shape[0]
    onehot = (ctf_groups[:, None] == jnp.arange(classes, dtype=jnp.int32)[None, :]).astype(
        jnp.float32
    )
    own = lax.dynamic_slice_in_dim(ctf_table, lax.axis_index("bas") * radii_dev, radii_dev, 1)
    weights = jnp.dot(onehot, own, precision=lax.Precision.HIGHEST)
    kept = (jnp.arange(kmax, dtype=jnp.int32)[None, :] < order_counts[:, None]).astype(jnp.float32)
    table = angular_table(jnp.arange(orders_dev * bas_size, dtype=jnp.int32), angles)
    weighted = (polar_images.astype(jnp.float32) * weights[:, :, None]).astype(jnp.bfloat16)
    spectra = jnp.einsum(
        "nt,tm->mn", weighted.reshape(-1, angles), table, preferred_element_type=jnp.float32
    ).astype(jnp.bfloat16)
    parts = spectra.reshape(bas_size, 2 * orders_dev, images_dev * radii_dev)
    parts = lax.all_to_all(parts, "bas", 0, 0, tiled=True)
    shaped = parts.reshape(bas_size, orders_dev, 2, images_dev, radii_dev)
    basis = radial_basis.reshape(orders_dev, bas_size, radii_dev, kmax)
    coeffs = jnp.einsum("sqcbr,qsrk->bqck", shaped, basis, preferred_element_type=jnp.float32)
    coeffs = (coeffs * kept[None, :, None, :]).astype(jnp.bfloat16)
    scale = 1.0 / (images_dev * img_size)
    full = jnp.einsum("bqck,bqcl->kql", coeffs, coeffs, preferred_element_type=jnp.float32)
    rows = kmax // img_size
    sent = full.astype(jnp.bfloat16).reshape(img_size, rows * orders_dev * kmax // 128, 128)
    got = lax.all_to_all(sent, "img", 0, 0, tiled=True)
    gram = jnp.sum(got.astype(jnp.float32), axis=0)
    return gram.reshape(rows, orders_dev * kmax) * scale


def solution(mesh):
    placed = (P("img", "bas", None), P("img"), P(), P("bas", None, None), P("bas"))
    return jax.shard_map(
        local, mesh=mesh, in_specs=placed, out_specs=P("img", "bas"), check_vma=False
    )
```

```python
import functools
import functools
import math

import jax
import jax.numpy as jnp
import ml_dtypes
import numpy as np
from jax import lax
from jax.experimental import pallas as pl
from jax.experimental.pallas import tpu as pltpu
from jax.sharding import PartitionSpec as P

F32, BF16 = jnp.float32, jnp.bfloat16
NT = (((1,), (1,)), ((), ()))


def angular_table(orders, angles):
    phase = np.arange(angles)[:, None] * np.arange(orders)[None, :] % angles
    theta = phase.astype(np.float32) * np.float32(2.0 * math.pi / angles)
    table = np.stack([np.cos(theta), np.sin(theta)], axis=-1) * np.float32(1.0 / math.sqrt(angles))
    table = table.reshape(angles // 8, 8, 2, orders).transpose(2, 0, 1, 3)
    return table.astype(ml_dtypes.bfloat16)


def transform(first_of, groups_in, ctf_in, images_in, table_in, parts_out, *scratch):
    groups, ctf, images, table, weighted, parts, sem_in, sem_out = scratch
    size, rows, lanes = parts.shape
    classes, radii = ctf.shape
    radii_dev = radii // size
    width = lanes // 2
    halves = table.shape[0]
    copies = [
        pltpu.make_async_copy(source, target, sem_in.at[n])
        for n, (source, target) in enumerate(
            [(groups_in, groups), (ctf_in, ctf), (images_in, images)]
            + [(table_in.at[n], table.at[n]) for n in range(halves)]
        )
    ]
    for copy in copies:
        copy.start()
    first = lax.axis_index("bas") * radii_dev
    shape = (radii_dev, radii)
    own = lax.broadcasted_iota(jnp.int32, shape, 1) == first + lax.broadcasted_iota(jnp.int32, shape, 0)
    copies[0].wait()
    copies[1].wait()

    def weight(i):
        row = ctf[pl.ds(groups[i], 1), :]
        return jnp.sum(jnp.where(own, row, 0.0), axis=1, keepdims=True)

    step = 16 // radii_dev
    scales = [
        jnp.concatenate([weight(i + j) for j in range(step)], axis=0)
        for i in range(0, groups.shape[0], step)
    ]
    copies[2].wait()
    for n, scale in enumerate(scales):
        block = slice(n * 16, (n + 1) * 16)
        weighted[block, :] = (images[block, :].astype(F32) * scale).astype(BF16)
    low = lax.broadcasted_iota(jnp.int32, (rows, lanes), 1) < width
    sends = []
    for half in range(halves):
        copies[3 + half].wait()
        columns = table[half].reshape(weighted.shape[1], -1)
        spectra = jnp.dot(weighted[...], columns, preferred_element_type=F32)
        for pair in range(columns.shape[1] // lanes):
            block = spectra[:, pair * lanes : (pair + 1) * lanes]
            one, two = block[:rows], block[rows:]
            turned_one, turned_two = pltpu.roll(one, width, 1), pltpu.roll(two, width, 1)
            for n, value in enumerate((jnp.where(low, one, turned_two), jnp.where(low, turned_one, two))):
                order = half * (size // halves) + 2 * pair + n
                place = (order - first_of) % size
                parts[place] = value.astype(BF16)
                send = pltpu.make_async_copy(parts.at[place], parts_out.at[place], sem_out.at[place])
                send.start()
                sends.append(send)
    for send in sends:
        send.wait()


def covariances(first_of, last_of, parts_ref, basis, out, by_order, staged):
    sources, rows, lanes = parts_ref.shape
    pairs, wide, radii = basis.shape
    radii_dev = radii // sources
    lows = rows // radii_dev
    width = lanes // 2
    half = wide // 2
    step = 16 // radii_dev
    for i in range(0, lows, step):
        block = parts_ref[:, i * radii_dev : (i + step) * radii_dev, :].astype(F32)
        for j in range(step):
            one = block[:, j * radii_dev : (j + 1) * radii_dev, :]
            one = jnp.concatenate([one[(n - first_of) % sources] for n in range(sources)], axis=0)
            by_order[(i + j) * lanes : (i + j + 1) * lanes, :] = one.T
    same = (lax.broadcasted_iota(jnp.int32, (wide, wide), 0) < half) == (
        lax.broadcasted_iota(jnp.int32, (wide, wide), 1) < half
    )
    for pair in range(pairs):
        rows_of = [
            by_order[pl.ds(high * width + 4 * pair + 2 * order + c, lows, stride=lanes), :]
            for order in range(2)
            for high in range(2)
            for c in range(2)
        ]
        spectra = jnp.concatenate(rows_of, axis=0).astype(BF16)
        coeffs = lax.dot_general(basis[pair], spectra, NT, preferred_element_type=F32)
        coeffs = jnp.where(same, coeffs, 0.0).astype(BF16)
        gram = lax.dot_general(coeffs, coeffs, NT, preferred_element_type=F32)
        staged[pl.ds(pair, half, stride=pairs), :] = gram[:half] + gram[half:]
    grams = staged[...].astype(BF16).reshape(out.shape)
    out[...] = grams
    if last_of:
        chunk = out.shape[0] // last_of[1]
        for here, there in ((0, last_of[0]), (last_of[0], 0)):
            out[here * chunk : (here + 1) * chunk] = grams[there * chunk : (there + 1) * chunk]


def local(table, polar_images, ctf_groups, ctf_table, radial_basis, order_counts):
    images_dev, radii_dev, angles = polar_images.shape
    orders_dev, radii, kmax = radial_basis.shape
    img_size, bas_size = lax.axis_size("img"), lax.axis_size("bas")
    hbm = pl.BlockSpec(memory_space=pltpu.HBM)
    vmem = pl.BlockSpec(memory_space=pltpu.VMEM)
    lows = images_dev // 2
    lanes = 4 * orders_dev
    shape = (bas_size, lows * radii_dev, lanes)
    first_of = bas_size // 2
    bas_order = [(n + first_of) % bas_size for n in range(bas_size)]
    images = polar_images.reshape(-1, angles)
    parts = pl.pallas_call(
        functools.partial(transform, first_of),
        out_shape=jax.ShapeDtypeStruct(shape, BF16),
        in_specs=[hbm] * 4,
        out_specs=hbm,
        scratch_shapes=[
            pltpu.SMEM(ctf_groups.shape, jnp.int32),
            pltpu.VMEM(ctf_table.shape, F32),
            pltpu.VMEM(images.shape, BF16),
            pltpu.VMEM(table.shape, BF16),
            pltpu.VMEM(images.shape, BF16),
            pltpu.VMEM(shape, BF16),
            pltpu.SemaphoreType.DMA((3 + table.shape[0],)),
            pltpu.SemaphoreType.DMA((bas_size,)),
        ],
        compiler_params=pltpu.CompilerParams(vmem_limit_bytes=60 * 2**20),
        name="transform",
    )(ctf_groups, ctf_table, images, table)
    parts, radial_basis, order_counts = lax.optimization_barrier((parts, radial_basis, order_counts))
    parts = lax.all_to_all(parts, "bas", 0, 0, tiled=True, axis_index_groups=[bas_order])
    kept = jnp.arange(kmax, dtype=jnp.int32)[None, :] < order_counts[:, None]
    basis = jnp.where(kept[:, None, :], radial_basis, jnp.zeros((), BF16))
    basis = basis.transpose(0, 2, 1).reshape(orders_dev // 2, 2 * kmax, radii)
    rows = kmax // img_size
    pairs = orders_dev // 2
    last = (5 * img_size // 8 + 1) % img_size
    img_order = list(range(img_size))
    img_order[0], img_order[last] = last, 0
    sent = pl.pallas_call(
        functools.partial(covariances, first_of, (last, img_size)),
        out_shape=jax.ShapeDtypeStruct((kmax, pairs, 2 * kmax), BF16),
        in_specs=[vmem, vmem],
        out_specs=vmem,
        scratch_shapes=[
            pltpu.VMEM((lows * lanes, radii), F32),
            pltpu.VMEM((kmax * pairs, 2 * kmax), F32),
        ],
        compiler_params=pltpu.CompilerParams(vmem_limit_bytes=16 * 2**20),
        name="covariances",
    )(parts, basis)
    sent = sent.reshape(img_size, rows * pairs, 2 * kmax)
    got = lax.all_to_all(sent, "img", 0, 0, tiled=True, axis_index_groups=[img_order])
    gram = jnp.sum(got.astype(F32), axis=0)
    return gram.reshape(rows, orders_dev * kmax) * (1.0 / (images_dev * img_size))


def solution(mesh):
    placed = (P("img", "bas", None), P("img"), P(), P("bas", None, None), P("bas"))

    def step(polar_images, ctf_groups, ctf_table, radial_basis, order_counts):
        table = jnp.asarray(angular_table(radial_basis.shape[0], polar_images.shape[2]))
        return jax.shard_map(
            local, mesh=mesh, in_specs=(P(),) + placed, out_specs=P("img", "bas"), check_vma=False
        )(table, polar_images, ctf_groups, ctf_table, radial_basis, order_counts)

    return step
```

```python
import functools
import functools
import math

import jax
import jax.numpy as jnp
import ml_dtypes
import numpy as np
from jax import lax
from jax.experimental import pallas as pl
from jax.experimental.pallas import tpu as pltpu
from jax.sharding import PartitionSpec as P

F32, BF16 = jnp.float32, jnp.bfloat16
NT = (((1,), (1,)), ((), ()))


def angular_table(orders, angles):
    phase = np.arange(angles)[:, None] * np.arange(orders)[None, :] % angles
    theta = phase.astype(np.float32) * np.float32(2.0 * math.pi / angles)
    table = np.stack([np.cos(theta), np.sin(theta)], axis=-1) * np.float32(1.0 / math.sqrt(angles))
    table = table.reshape(angles // 8, 8, 2, orders).transpose(2, 0, 1, 3)
    return table.astype(ml_dtypes.bfloat16)


def transform(place_of, groups_in, ctf_in, images_in, table_in, parts_out, *scratch):
    groups, ctf, images, table, weighted, parts, sem_in, sem_out = scratch
    size, rows, lanes = parts.shape
    classes, radii = ctf.shape
    radii_dev = weighted.shape[0] // groups.shape[0]
    highs = weighted.shape[0] // rows
    width = lanes // highs
    halves = table.shape[0]
    copies = [
        pltpu.make_async_copy(source, target, sem_in.at[n])
        for n, (source, target) in enumerate(
            [(groups_in, groups), (ctf_in, ctf), (images_in, images)]
            + [(table_in.at[n], table.at[n]) for n in range(halves)]
        )
    ]
    for copy in copies:
        copy.start()
    first = lax.axis_index("bas") * radii_dev
    shape = (radii_dev, radii)
    own = lax.broadcasted_iota(jnp.int32, shape, 1) == first + lax.broadcasted_iota(jnp.int32, shape, 0)
    copies[0].wait()
    copies[1].wait()

    def weight(i):
        row = ctf[pl.ds(groups[i], 1), :]
        return jnp.sum(jnp.where(own, row, 0.0), axis=1, keepdims=True)

    step = 16 // radii_dev
    scales = [
        jnp.concatenate([weight(i + j) for j in range(step)], axis=0)
        for i in range(0, groups.shape[0], step)
    ]
    copies[2].wait()
    for n, scale in enumerate(scales):
        block = slice(n * 16, (n + 1) * 16)
        weighted[block, :] = (images[block, :].astype(F32) * scale).astype(BF16)
    group = lax.broadcasted_iota(jnp.int32, (rows, lanes), 1) // width
    for half in range(halves):
        copies[3 + half].wait()
    for half in range(halves):
        columns = table[half].reshape(weighted.shape[1], -1)
        spectra = jnp.dot(weighted[...], columns, preferred_element_type=F32)
        tiles = columns.shape[1] // lanes
        for tile in range(tiles):
            part = spectra[:, tile * lanes : (tile + 1) * lanes]
            blocks = [part[n * rows : (n + 1) * rows] for n in range(highs)]
            shift = highs // 2
            while shift:
                keep = (group & shift) == 0
                for n in range(highs):
                    if not n & shift:
                        one, two = blocks[n], blocks[n + shift]
                        turned_one = pltpu.roll(one, lanes - shift * width, 1)
                        turned_two = pltpu.roll(two, shift * width, 1)
                        blocks[n] = jnp.where(keep, one, turned_two)
                        blocks[n + shift] = jnp.where(keep, turned_one, two)
                shift //= 2
            for n, value in enumerate(blocks):
                place = place_of[(half * tiles + tile) * highs + n]
                parts[place] = value.astype(BF16)
    send = pltpu.make_async_copy(parts, parts_out, sem_out.at[0])
    send.start()
    send.wait()


def covariances(place_of, last_of, parts_ref, basis, out, by_order, staged):
    places, rows, lanes = parts_ref.shape
    pairs, wide, radii = basis.shape
    pool = len(place_of[0])
    sources = places // pool
    radii_dev = radii // sources
    lows = rows // radii_dev
    width = 4 * pairs
    highs = lanes // width
    half = wide // 2
    step = 16 // radii_dev
    blocks = pool * lows
    for i in range(0, lows, step):
        block = parts_ref[:, i * radii_dev : (i + step) * radii_dev, :].astype(F32)
        for j in range(step):
            for sub in range(pool):
                at = slice(j * radii_dev, (j + 1) * radii_dev)
                one = jnp.concatenate([block[place_of[n][sub]][at] for n in range(sources)], axis=0)
                n = (sub * lows + i + j) * lanes
                by_order[n : n + lanes, :] = one.T
    samples = 2 * highs * blocks
    shape = (wide, 2 * samples)
    same = (lax.broadcasted_iota(jnp.int32, shape, 0) < half) == (
        lax.broadcasted_iota(jnp.int32, shape, 1) < samples
    )
    for pair in range(pairs):
        rows_of = [
            by_order[pl.ds(high * width + 4 * pair + 2 * order + c, blocks, stride=lanes), :]
            for order in range(2)
            for high in range(highs)
            for c in range(2)
        ]
        spectra = jnp.concatenate(rows_of, axis=0).astype(BF16)
        coeffs = lax.dot_general(basis[pair], spectra, NT, preferred_element_type=F32)
        coeffs = jnp.where(same, coeffs, 0.0).astype(BF16)
        gram = lax.dot_general(coeffs, coeffs, NT, preferred_element_type=F32)
        staged[pl.ds(pair, half, stride=pairs), :] = gram[:half] + gram[half:]
    grams = staged[...].astype(BF16).reshape(out.shape)
    out[...] = grams
    if last_of:
        chunk = out.shape[0] // last_of[1]
        for here, there in ((0, last_of[0]), (last_of[0], 0)):
            out[here * chunk : (here + 1) * chunk] = grams[there * chunk : (there + 1) * chunk]


def local(table, polar_images, ctf_groups, ctf_table, radial_basis, order_counts):
    images_dev, radii_dev, angles = polar_images.shape
    orders_dev, radii, kmax = radial_basis.shape
    img_size, bas_size = lax.axis_size("img"), lax.axis_size("bas")
    hbm = pl.BlockSpec(memory_space=pltpu.HBM)
    vmem = pl.BlockSpec(memory_space=pltpu.VMEM)
    pool = 2
    lanes = 128
    lows = images_dev * orders_dev * 2 // pool // lanes
    places = bas_size * pool
    shape = (places, lows * radii_dev, lanes)
    ring = [(high, sub, core) for high in range(bas_size // 2) for sub in range(pool) for core in range(2)]
    start = places // 2
    ring = ring[start:] + ring[:start]
    members = [(sub, 2 * high + core) for high, sub, core in ring]
    place_of = [[members.index((sub, bas)) for sub in range(pool)] for bas in range(bas_size)]
    teams = [
        [(team * pool + sub) * bas_size + bas for sub, bas in members] for team in range(img_size // pool)
    ]
    images = polar_images.reshape(-1, angles)
    parts = pl.pallas_call(
        functools.partial(transform, sum(place_of, [])),
        out_shape=jax.ShapeDtypeStruct(shape, BF16),
        in_specs=[hbm] * 4,
        out_specs=hbm,
        scratch_shapes=[
            pltpu.SMEM(ctf_groups.shape, jnp.int32),
            pltpu.VMEM(ctf_table.shape, F32),
            pltpu.VMEM(images.shape, BF16),
            pltpu.VMEM(table.shape, BF16),
            pltpu.VMEM(images.shape, BF16),
            pltpu.VMEM(shape, BF16),
            pltpu.SemaphoreType.DMA((3 + table.shape[0],)),
            pltpu.SemaphoreType.DMA((1,)),
        ],
        compiler_params=pltpu.CompilerParams(vmem_limit_bytes=60 * 2**20),
        name="transform",
    )(ctf_groups, ctf_table, images, table)
    parts, radial_basis, order_counts = lax.optimization_barrier((parts, radial_basis, order_counts))
    parts = lax.all_to_all(parts, ("img", "bas"), 0, 0, tiled=True, axis_index_groups=teams)
    orders = orders_dev // pool
    mine = lax.axis_index("img") % pool * orders
    counts = lax.dynamic_slice_in_dim(order_counts, mine, orders)
    basis = lax.dynamic_slice_in_dim(radial_basis, mine, orders)
    kept = jnp.arange(kmax, dtype=jnp.int32)[None, :] < counts[:, None]
    basis = jnp.where(kept[:, None, :], basis, jnp.zeros((), BF16))
    basis = basis.transpose(0, 2, 1).reshape(orders // 2, 2 * kmax, radii)
    rows = kmax // img_size
    pairs = orders // 2
    last = img_size // 64 * 42
    img_order = list(range(img_size))
    img_order[0], img_order[last] = last, 0
    sent = pl.pallas_call(
        functools.partial(covariances, place_of, (last, img_size)),
        out_shape=jax.ShapeDtypeStruct((kmax, pairs, 2 * kmax), BF16),
        in_specs=[vmem, vmem],
        out_specs=vmem,
        scratch_shapes=[
            pltpu.VMEM((pool * lows * lanes, radii), F32),
            pltpu.VMEM((kmax * pairs, 2 * kmax), F32),
        ],
        compiler_params=pltpu.CompilerParams(vmem_limit_bytes=16 * 2**20),
        name="covariances",
    )(parts, basis)
    sent = sent.reshape(img_size, rows * pairs, 2 * kmax)
    got = lax.all_to_all(sent, "img", 0, 0, tiled=True, axis_index_groups=[img_order])
    got = got.astype(F32).reshape(img_size // pool, pool, rows, pairs, 2 * kmax)
    gram = jnp.sum(got, axis=0).swapaxes(0, 1)
    return gram.reshape(rows, orders_dev * kmax) * (1.0 / (images_dev * img_size))


def solution(mesh):
    placed = (P("img", "bas", None), P("img"), P(), P("bas", None, None), P("bas"))

    def step(polar_images, ctf_groups, ctf_table, radial_basis, order_counts):
        table = jnp.asarray(angular_table(radial_basis.shape[0], polar_images.shape[2]))
        return jax.shard_map(
            local, mesh=mesh, in_specs=(P(),) + placed, out_specs=P("img", "bas"), check_vma=False
        )(table, polar_images, ctf_groups, ctf_table, radial_basis, order_counts)

    return step
```

```python
import functools
import functools
import math

import jax
import jax.numpy as jnp
import ml_dtypes
import numpy as np
from jax import lax
from jax.experimental import pallas as pl
from jax.experimental.pallas import tpu as pltpu
from jax.sharding import PartitionSpec as P

F32, BF16 = jnp.float32, jnp.bfloat16
NT = (((1,), (1,)), ((), ()))


def angular_table(orders, angles):
    phase = np.arange(angles)[:, None] * np.arange(orders)[None, :] % angles
    theta = phase.astype(np.float32) * np.float32(2.0 * math.pi / angles)
    table = np.stack([np.cos(theta), np.sin(theta)], axis=-1) * np.float32(1.0 / math.sqrt(angles))
    table = table.reshape(angles // 8, 8, 2, orders).transpose(2, 0, 1, 3)
    return table.astype(ml_dtypes.bfloat16)


def transform(place_of, groups_in, ctf_in, images_in, table_in, parts_out, *scratch):
    groups, ctf, images, table, weighted, parts, sem_in, sem_out = scratch
    size, rows, lanes = parts.shape
    classes, radii = ctf.shape
    radii_dev = weighted.shape[0] // groups.shape[0]
    highs = weighted.shape[0] // rows
    width = lanes // highs
    halves = table.shape[0]
    copies = [
        pltpu.make_async_copy(source, target, sem_in.at[n])
        for n, (source, target) in enumerate(
            [(groups_in, groups), (ctf_in, ctf), (images_in, images)]
            + [(table_in.at[n], table.at[n]) for n in range(halves)]
        )
    ]
    for copy in copies:
        copy.start()
    first = lax.axis_index("bas") * radii_dev
    shape = (radii_dev, radii)
    own = lax.broadcasted_iota(jnp.int32, shape, 1) == first + lax.broadcasted_iota(jnp.int32, shape, 0)
    copies[0].wait()
    copies[1].wait()

    def weight(i):
        row = ctf[pl.ds(groups[i], 1), :]
        return jnp.sum(jnp.where(own, row, 0.0), axis=1, keepdims=True)

    step = 16 // radii_dev
    scales = [
        jnp.concatenate([weight(i + j) for j in range(step)], axis=0)
        for i in range(0, groups.shape[0], step)
    ]
    copies[2].wait()
    for n, scale in enumerate(scales):
        block = slice(n * 16, (n + 1) * 16)
        weighted[block, :] = (images[block, :].astype(F32) * scale).astype(BF16)
    group = lax.broadcasted_iota(jnp.int32, (rows, lanes), 1) // width
    for half in range(halves):
        copies[3 + half].wait()
    for half in range(halves):
        columns = table[half].reshape(weighted.shape[1], -1)
        spectra = jnp.dot(weighted[...], columns, preferred_element_type=F32)
        tiles = columns.shape[1] // lanes
        for tile in range(tiles):
            part = spectra[:, tile * lanes : (tile + 1) * lanes]
            blocks = [part[n * rows : (n + 1) * rows] for n in range(highs)]
            shift = highs // 2
            while shift:
                keep = (group & shift) == 0
                for n in range(highs):
                    if not n & shift:
                        one, two = blocks[n], blocks[n + shift]
                        turned_one = pltpu.roll(one, lanes - shift * width, 1)
                        turned_two = pltpu.roll(two, shift * width, 1)
                        blocks[n] = jnp.where(keep, one, turned_two)
                        blocks[n + shift] = jnp.where(keep, turned_one, two)
                shift //= 2
            for n, value in enumerate(blocks):
                place = place_of[(half * tiles + tile) * highs + n]
                parts[place] = value.astype(BF16)
    send = pltpu.make_async_copy(parts, parts_out, sem_out.at[0])
    send.start()
    send.wait()


def covariances(place_of, chunk_of, parts_ref, basis, out, by_order, staged):
    places, rows, lanes = parts_ref.shape
    pairs, wide, radii = basis.shape
    pool = len(place_of[0])
    sources = places // pool
    radii_dev = radii // sources
    lows = rows // radii_dev
    width = 4 * pairs
    highs = lanes // width
    half = wide // 2
    step = 16 // radii_dev
    blocks = pool * lows
    for i in range(0, lows, step):
        block = parts_ref[:, i * radii_dev : (i + step) * radii_dev, :].astype(F32)
        for j in range(step):
            for sub in range(pool):
                at = slice(j * radii_dev, (j + 1) * radii_dev)
                one = jnp.concatenate([block[place_of[n][sub]][at] for n in range(sources)], axis=0)
                n = (sub * lows + i + j) * lanes
                by_order[n : n + lanes, :] = one.T
    samples = 2 * highs * blocks
    shape = (wide, 2 * samples)
    same = (lax.broadcasted_iota(jnp.int32, shape, 0) < half) == (
        lax.broadcasted_iota(jnp.int32, shape, 1) < samples
    )
    for pair in range(pairs):
        rows_of = [
            by_order[pl.ds(high * width + 4 * pair + 2 * order + c, blocks, stride=lanes), :]
            for order in range(2)
            for high in range(highs)
            for c in range(2)
        ]
        spectra = jnp.concatenate(rows_of, axis=0).astype(BF16)
        coeffs = lax.dot_general(basis[pair], spectra, NT, preferred_element_type=F32)
        coeffs = jnp.where(same, coeffs, 0.0).astype(BF16)
        gram = lax.dot_general(coeffs, coeffs, NT, preferred_element_type=F32)
        staged[pl.ds(pair, half, stride=pairs), :] = gram[:half] + gram[half:]
    count = len(chunk_of)
    chunk = out.shape[0] // count
    for here in range(count):
        out[here * chunk : (here + 1) * chunk, :] = staged[chunk_of[here] * chunk : (chunk_of[here] + 1) * chunk, :]


def local(table, polar_images, ctf_groups, ctf_table, radial_basis, order_counts):
    images_dev, radii_dev, angles = polar_images.shape
    orders_dev, radii, kmax = radial_basis.shape
    img_size, bas_size = lax.axis_size("img"), lax.axis_size("bas")
    hbm = pl.BlockSpec(memory_space=pltpu.HBM)
    vmem = pl.BlockSpec(memory_space=pltpu.VMEM)
    pool = 4
    lanes = 128
    lows = images_dev * orders_dev * 2 // pool // lanes
    places = bas_size * pool
    shape = (places, lows * radii_dev, lanes)
    ring = [(high, sub, core) for high in range(bas_size // 2) for sub in range(pool) for core in range(2)]
    start = 5 * places // 8
    ring = ring[start:] + ring[:start]
    members = [(sub, 2 * high + core) for high, sub, core in ring]
    place_of = [[members.index((sub, bas)) for sub in range(pool)] for bas in range(bas_size)]
    teams = [
        [(team * pool + sub) * bas_size + bas for sub, bas in members] for team in range(img_size // pool)
    ]
    images = polar_images.reshape(-1, angles)
    parts = pl.pallas_call(
        functools.partial(transform, sum(place_of, [])),
        out_shape=jax.ShapeDtypeStruct(shape, BF16),
        in_specs=[hbm] * 4,
        out_specs=hbm,
        scratch_shapes=[
            pltpu.SMEM(ctf_groups.shape, jnp.int32),
            pltpu.VMEM(ctf_table.shape, F32),
            pltpu.VMEM(images.shape, BF16),
            pltpu.VMEM(table.shape, BF16),
            pltpu.VMEM(images.shape, BF16),
            pltpu.VMEM(shape, BF16),
            pltpu.SemaphoreType.DMA((3 + table.shape[0],)),
            pltpu.SemaphoreType.DMA((1,)),
        ],
        compiler_params=pltpu.CompilerParams(vmem_limit_bytes=60 * 2**20),
        name="transform",
    )(ctf_groups, ctf_table, images, table)
    parts, radial_basis, order_counts = lax.optimization_barrier((parts, radial_basis, order_counts))
    parts = lax.all_to_all(parts, ("img", "bas"), 0, 0, tiled=True, axis_index_groups=teams)
    orders = orders_dev // pool
    mine = lax.axis_index("img") % pool * orders
    counts = lax.dynamic_slice_in_dim(order_counts, mine, orders)
    basis = lax.dynamic_slice_in_dim(radial_basis, mine, orders)
    kept = jnp.arange(kmax, dtype=jnp.int32)[None, :] < counts[:, None]
    basis = jnp.where(kept[:, None, :], basis, jnp.zeros((), BF16))
    basis = basis.transpose(0, 2, 1).reshape(orders // 2, 2 * kmax, radii)
    rows = kmax // img_size
    pairs = orders // 2
    img_order = [n ^ (img_size // 64 * 42) for n in range(img_size)]
    sent = pl.pallas_call(
        functools.partial(covariances, place_of, img_order),
        out_shape=jax.ShapeDtypeStruct((kmax * pairs, 2 * kmax), F32),
        in_specs=[vmem, vmem],
        out_specs=vmem,
        scratch_shapes=[
            pltpu.VMEM((pool * lows * lanes, radii), F32),
            pltpu.VMEM((kmax * pairs, 2 * kmax), F32),
        ],
        compiler_params=pltpu.CompilerParams(vmem_limit_bytes=16 * 2**20),
        name="covariances",
    )(parts, basis)
    sent = sent.reshape(img_size, rows * pairs, 2 * kmax)
    got = lax.all_to_all(sent, "img", 0, 0, tiled=True, axis_index_groups=[img_order])
    gram = jnp.sum(got.reshape(img_size // pool, pool, rows, pairs, 2 * kmax), axis=0)
    gram = jnp.stack([gram[img_order[n] % pool] for n in range(pool)], axis=1)
    return gram.reshape(rows, orders_dev * kmax) * (1.0 / (images_dev * img_size))


def solution(mesh):
    placed = (P("img", "bas", None), P("img"), P(), P("bas", None, None), P("bas"))

    def step(polar_images, ctf_groups, ctf_table, radial_basis, order_counts):
        table = jnp.asarray(angular_table(radial_basis.shape[0], polar_images.shape[2]))
        return jax.shard_map(
            local, mesh=mesh, in_specs=(P(),) + placed, out_specs=P("img", "bas"), check_vma=False
        )(table, polar_images, ctf_groups, ctf_table, radial_basis, order_counts)

    return step
```

```python
import functools
import functools
import math

import jax
import jax.numpy as jnp
import ml_dtypes
import numpy as np
from jax import lax
from jax.experimental import pallas as pl
from jax.experimental.pallas import tpu as pltpu
from jax.sharding import PartitionSpec as P

F32, BF16 = jnp.float32, jnp.bfloat16
NT = (((1,), (1,)), ((), ()))


def angular_table(orders, angles):
    phase = np.arange(angles)[:, None] * np.arange(orders)[None, :] % angles
    theta = phase.astype(np.float32) * np.float32(2.0 * math.pi / angles)
    table = np.stack([np.cos(theta), np.sin(theta)], axis=-1) * np.float32(1.0 / math.sqrt(angles))
    table = table.reshape(angles // 8, 8, 2, orders).transpose(2, 0, 1, 3)
    return table.astype(ml_dtypes.bfloat16)


def transform(place_of, groups_in, ctf_in, images_in, table_in, parts_out, *scratch):
    groups, ctf, images, table, weighted, parts, sem_in, sem_out = scratch
    size, rows, lanes = parts.shape
    classes, radii = ctf.shape
    radii_dev = weighted.shape[0] // groups.shape[0]
    highs = weighted.shape[0] // rows
    width = lanes // highs
    halves = table.shape[0]
    copies = [
        pltpu.make_async_copy(source, target, sem_in.at[n])
        for n, (source, target) in enumerate(
            [(groups_in, groups), (ctf_in, ctf), (images_in, images)]
            + [(table_in.at[n], table.at[n]) for n in range(halves)]
        )
    ]
    for copy in copies:
        copy.start()
    first = lax.axis_index("bas") * radii_dev
    shape = (radii_dev, radii)
    own = lax.broadcasted_iota(jnp.int32, shape, 1) == first + lax.broadcasted_iota(jnp.int32, shape, 0)
    copies[0].wait()
    copies[1].wait()

    def weight(i):
        row = ctf[pl.ds(groups[i], 1), :]
        return jnp.sum(jnp.where(own, row, 0.0), axis=1, keepdims=True)

    step = 16 // radii_dev
    scales = [
        jnp.concatenate([weight(i + j) for j in range(step)], axis=0)
        for i in range(0, groups.shape[0], step)
    ]
    copies[2].wait()
    for n, scale in enumerate(scales):
        block = slice(n * 16, (n + 1) * 16)
        weighted[block, :] = (images[block, :].astype(F32) * scale).astype(BF16)
    group = lax.broadcasted_iota(jnp.int32, (rows, lanes), 1) // width
    for half in range(halves):
        copies[3 + half].wait()
    for half in range(halves):
        columns = table[half].reshape(weighted.shape[1], -1)
        spectra = jnp.dot(weighted[...], columns, preferred_element_type=F32)
        tiles = columns.shape[1] // lanes
        for tile in range(tiles):
            part = spectra[:, tile * lanes : (tile + 1) * lanes]
            blocks = [part[n * rows : (n + 1) * rows] for n in range(highs)]
            shift = highs // 2
            while shift:
                keep = (group & shift) == 0
                for n in range(highs):
                    if not n & shift:
                        one, two = blocks[n], blocks[n + shift]
                        turned_one = pltpu.roll(one, lanes - shift * width, 1)
                        turned_two = pltpu.roll(two, shift * width, 1)
                        blocks[n] = jnp.where(keep, one, turned_two)
                        blocks[n + shift] = jnp.where(keep, turned_one, two)
                shift //= 2
            for n, value in enumerate(blocks):
                place = place_of[(half * tiles + tile) * highs + n]
                parts[place] = value.astype(BF16)
    send = pltpu.make_async_copy(parts, parts_out, sem_out.at[0])
    send.start()
    send.wait()


def covariances(place_of, chunk_of, parts_ref, basis, out, by_order, staged):
    places, rows, lanes = parts_ref.shape
    pairs, wide, radii = basis.shape
    pool = len(place_of[0])
    sources = places // pool
    radii_dev = radii // sources
    lows = rows // radii_dev
    width = 4 * pairs
    highs = lanes // width
    half = wide // 2
    step = 16 // radii_dev
    blocks = pool * lows
    for i in range(0, lows, step):
        block = parts_ref[:, i * radii_dev : (i + step) * radii_dev, :].astype(F32)
        for j in range(step):
            for sub in range(pool):
                at = slice(j * radii_dev, (j + 1) * radii_dev)
                one = jnp.concatenate([block[place_of[n][sub]][at] for n in range(sources)], axis=0)
                n = (sub * lows + i + j) * lanes
                by_order[n : n + lanes, :] = one.T
    samples = 2 * highs * blocks
    shape = (wide, 2 * samples)
    same = (lax.broadcasted_iota(jnp.int32, shape, 0) < half) == (
        lax.broadcasted_iota(jnp.int32, shape, 1) < samples
    )
    for pair in range(pairs):
        rows_of = [
            by_order[pl.ds(high * width + 4 * pair + 2 * order + c, blocks, stride=lanes), :]
            for order in range(2)
            for high in range(highs)
            for c in range(2)
        ]
        spectra = jnp.concatenate(rows_of, axis=0).astype(BF16)
        coeffs = lax.dot_general(basis[pair], spectra, NT, preferred_element_type=F32)
        coeffs = jnp.where(same, coeffs, 0.0).astype(BF16)
        gram = lax.dot_general(coeffs, coeffs, NT, preferred_element_type=F32)
        staged[pl.ds(pair, half, stride=pairs), :] = gram[:half] + gram[half:]
    count = len(chunk_of) // 2
    step = out.shape[0] // count
    for here in range(count):
        there = chunk_of[2 * here] // 2
        out[here * step : (here + 1) * step, :] = staged[there * step : (there + 1) * step, :]


def local(table, polar_images, ctf_groups, ctf_table, radial_basis, order_counts):
    images_dev, radii_dev, angles = polar_images.shape
    orders_dev, radii, kmax = radial_basis.shape
    img_size, bas_size = lax.axis_size("img"), lax.axis_size("bas")
    hbm = pl.BlockSpec(memory_space=pltpu.HBM)
    vmem = pl.BlockSpec(memory_space=pltpu.VMEM)
    pool = 4
    lanes = 128
    lows = images_dev * orders_dev * 2 // pool // lanes
    places = bas_size * pool
    shape = (places, lows * radii_dev, lanes)
    ring = [(high, sub, core) for high in range(bas_size // 2) for sub in range(pool) for core in range(2)]
    start = 5 * places // 8
    ring = ring[start:] + ring[:start]
    members = [(sub, 2 * high + core) for high, sub, core in ring]
    place_of = [[members.index((sub, bas)) for sub in range(pool)] for bas in range(bas_size)]
    teams = [
        [(team * pool + sub) * bas_size + bas for sub, bas in members] for team in range(img_size // pool)
    ]
    images = polar_images.reshape(-1, angles)
    parts = pl.pallas_call(
        functools.partial(transform, sum(place_of, [])),
        out_shape=jax.ShapeDtypeStruct(shape, BF16),
        in_specs=[hbm] * 4,
        out_specs=hbm,
        scratch_shapes=[
            pltpu.SMEM(ctf_groups.shape, jnp.int32),
            pltpu.VMEM(ctf_table.shape, F32),
            pltpu.VMEM(images.shape, BF16),
            pltpu.VMEM(table.shape, BF16),
            pltpu.VMEM(images.shape, BF16),
            pltpu.VMEM(shape, BF16),
            pltpu.SemaphoreType.DMA((3 + table.shape[0],)),
            pltpu.SemaphoreType.DMA((1,)),
        ],
        compiler_params=pltpu.CompilerParams(vmem_limit_bytes=60 * 2**20),
        name="transform",
    )(ctf_groups, ctf_table, images, table)
    parts, radial_basis, order_counts = lax.optimization_barrier((parts, radial_basis, order_counts))
    parts = lax.all_to_all(parts, ("img", "bas"), 0, 0, tiled=True, axis_index_groups=teams)
    orders = orders_dev // pool
    mine = lax.axis_index("img") % pool * orders
    counts = lax.dynamic_slice_in_dim(order_counts, mine, orders)
    basis = lax.dynamic_slice_in_dim(radial_basis, mine, orders)
    kept = jnp.arange(kmax, dtype=jnp.int32)[None, :] < counts[:, None]
    basis = jnp.where(kept[:, None, :], basis, jnp.zeros((), BF16))
    basis = basis.transpose(0, 2, 1).reshape(orders // 2, 2 * kmax, radii)
    rows = kmax // img_size
    pairs = orders // 2
    img_order = [n ^ (img_size // 64 * 42) for n in range(img_size)]
    sent = pl.pallas_call(
        functools.partial(covariances, place_of, img_order),
        out_shape=jax.ShapeDtypeStruct((kmax * pairs, 2 * kmax), F32),
        in_specs=[vmem, vmem],
        out_specs=vmem,
        scratch_shapes=[
            pltpu.VMEM(((pool * lows + 1) * lanes, radii), F32),
            pltpu.VMEM((kmax * pairs + 8, 2 * kmax), F32),
        ],
        compiler_params=pltpu.CompilerParams(vmem_limit_bytes=16 * 2**20),
        name="covariances",
    )(parts, basis)
    sent = sent.reshape(img_size, rows * pairs, 2 * kmax)
    got = lax.all_to_all(sent, "img", 0, 0, tiled=True, axis_index_groups=[img_order])
    gram = jnp.sum(got.reshape(img_size // pool, pool, rows, pairs, 2 * kmax), axis=0)
    gram = jnp.stack([gram[img_order[n] % pool] for n in range(pool)], axis=1)
    return gram.reshape(rows, orders_dev * kmax) * (1.0 / (images_dev * img_size))


def solution(mesh):
    placed = (P("img", "bas", None), P("img"), P(), P("bas", None, None), P("bas"))

    def step(polar_images, ctf_groups, ctf_table, radial_basis, order_counts):
        table = jnp.asarray(angular_table(radial_basis.shape[0], polar_images.shape[2]))
        return jax.shard_map(
            local, mesh=mesh, in_specs=(P(),) + placed, out_specs=P("img", "bas"), check_vma=False
        )(table, polar_images, ctf_groups, ctf_table, radial_basis, order_counts)

    return step
```

```python
import functools
import functools
import math

import jax
import jax.numpy as jnp
import ml_dtypes
import numpy as np
from jax import lax
from jax.experimental import pallas as pl
from jax.experimental.pallas import tpu as pltpu
from jax.sharding import PartitionSpec as P

F32, BF16 = jnp.float32, jnp.bfloat16
NT = (((1,), (1,)), ((), ()))


def angular_table(orders, angles):
    phase = np.arange(angles)[:, None] * np.arange(orders)[None, :] % angles
    theta = phase.astype(np.float32) * np.float32(2.0 * math.pi / angles)
    table = np.stack([np.cos(theta), np.sin(theta)], axis=-1) * np.float32(1.0 / math.sqrt(angles))
    table = table.reshape(angles // 8, 8, 2, orders).transpose(2, 0, 1, 3)
    return table.astype(ml_dtypes.bfloat16)


def transform(place_of, groups_in, ctf_in, images_in, table_in, parts_out, *scratch):
    groups, ctf, images, table, weighted, parts, sem_in, sem_out = scratch
    size, rows, lanes = parts.shape
    classes, radii = ctf.shape
    radii_dev = weighted.shape[0] // groups.shape[0]
    highs = weighted.shape[0] // rows
    width = lanes // highs
    halves = table.shape[0]
    copies = [
        pltpu.make_async_copy(source, target, sem_in.at[n])
        for n, (source, target) in enumerate(
            [(groups_in, groups), (ctf_in, ctf), (images_in, images)]
            + [(table_in.at[n], table.at[n]) for n in range(halves)]
        )
    ]
    for copy in copies:
        copy.start()
    first = lax.axis_index("bas") * radii_dev
    shape = (radii_dev, radii)
    own = lax.broadcasted_iota(jnp.int32, shape, 1) == first + lax.broadcasted_iota(jnp.int32, shape, 0)
    copies[0].wait()
    copies[1].wait()

    def weight(i):
        row = ctf[pl.ds(groups[i], 1), :]
        return jnp.sum(jnp.where(own, row, 0.0), axis=1, keepdims=True)

    step = 16 // radii_dev
    scales = [
        jnp.concatenate([weight(i + j) for j in range(step)], axis=0)
        for i in range(0, groups.shape[0], step)
    ]
    copies[2].wait()
    for n, scale in enumerate(scales):
        block = slice(n * 16, (n + 1) * 16)
        weighted[block, :] = (images[block, :].astype(F32) * scale).astype(BF16)
    group = lax.broadcasted_iota(jnp.int32, (rows, lanes), 1) // width
    for half in range(halves):
        copies[3 + half].wait()
    sends = []
    for half in range(halves):
        columns = table[half].reshape(weighted.shape[1], -1)
        spectra = jnp.dot(weighted[...], columns, preferred_element_type=F32)
        tiles = columns.shape[1] // lanes
        for tile in range(tiles):
            part = spectra[:, tile * lanes : (tile + 1) * lanes]
            blocks = [part[n * rows : (n + 1) * rows] for n in range(highs)]
            shift = highs // 2
            while shift:
                keep = (group & shift) == 0
                for n in range(highs):
                    if not n & shift:
                        one, two = blocks[n], blocks[n + shift]
                        turned_one = pltpu.roll(one, lanes - shift * width, 1)
                        turned_two = pltpu.roll(two, shift * width, 1)
                        blocks[n] = jnp.where(keep, one, turned_two)
                        blocks[n + shift] = jnp.where(keep, turned_one, two)
                shift //= 2
            for n, value in enumerate(blocks):
                place = place_of[(half * tiles + tile) * highs + n]
                parts[place] = value.astype(BF16)
        span = size // halves
        begin = min(place_of[half * span : (half + 1) * span])
        send = pltpu.make_async_copy(
            parts.at[pl.ds(begin, span)], parts_out.at[pl.ds(begin, span)], sem_out.at[half]
        )
        send.start()
        sends.append(send)
    for send in sends:
        send.wait()


def covariances(place_of, chunk_of, parts_ref, basis, out, by_order, staged):
    places, rows, lanes = parts_ref.shape
    pairs, wide, radii = basis.shape
    pool = len(place_of[0])
    sources = places // pool
    radii_dev = radii // sources
    lows = rows // radii_dev
    width = 4 * pairs
    highs = lanes // width
    half = wide // 2
    step = 16 // radii_dev
    blocks = pool * lows
    for i in range(0, lows, step):
        block = parts_ref[:, i * radii_dev : (i + step) * radii_dev, :].astype(F32)
        for j in range(step):
            for sub in range(pool):
                at = slice(j * radii_dev, (j + 1) * radii_dev)
                one = jnp.concatenate([block[place_of[n][sub]][at] for n in range(sources)], axis=0)
                n = (sub * lows + i + j) * lanes
                by_order[n : n + lanes, :] = one.T
    samples = 2 * highs * blocks
    shape = (wide, 2 * samples)
    same = (lax.broadcasted_iota(jnp.int32, shape, 0) < half) == (
        lax.broadcasted_iota(jnp.int32, shape, 1) < samples
    )
    for pair in range(pairs):
        rows_of = [
            by_order[pl.ds(high * width + 4 * pair + 2 * order + c, blocks, stride=lanes), :]
            for order in range(2)
            for high in range(highs)
            for c in range(2)
        ]
        spectra = jnp.concatenate(rows_of, axis=0).astype(BF16)
        coeffs = lax.dot_general(basis[pair], spectra, NT, preferred_element_type=F32)
        coeffs = jnp.where(same, coeffs, 0.0).astype(BF16)
        gram = lax.dot_general(coeffs, coeffs, NT, preferred_element_type=F32)
        staged[pl.ds(pair, half, stride=pairs), :] = gram[:half] + gram[half:]
    count = len(chunk_of) // 2
    step = out.shape[0] // count
    for here in range(count):
        there = chunk_of[2 * here] // 2
        out[here * step : (here + 1) * step, :] = staged[there * step : (there + 1) * step, :]


def local(table, polar_images, ctf_groups, ctf_table, radial_basis, order_counts):
    images_dev, radii_dev, angles = polar_images.shape
    orders_dev, radii, kmax = radial_basis.shape
    img_size, bas_size = lax.axis_size("img"), lax.axis_size("bas")
    hbm = pl.BlockSpec(memory_space=pltpu.HBM)
    vmem = pl.BlockSpec(memory_space=pltpu.VMEM)
    pool = 4
    lanes = 128
    lows = images_dev * orders_dev * 2 // pool // lanes
    places = bas_size * pool
    shape = (places, lows * radii_dev, lanes)
    ring = [(high, sub, core) for high in range(bas_size // 2) for sub in range(pool) for core in range(2)]
    start = places // 2
    ring = ring[start:] + ring[:start]
    members = [(sub, 2 * high + core) for high, sub, core in ring]
    place_of = [[members.index((sub, bas)) for sub in range(pool)] for bas in range(bas_size)]
    teams = [
        [(team * pool + sub) * bas_size + bas for sub, bas in members] for team in range(img_size // pool)
    ]
    images = polar_images.reshape(-1, angles)
    parts = pl.pallas_call(
        functools.partial(transform, sum(place_of, [])),
        out_shape=jax.ShapeDtypeStruct(shape, BF16),
        in_specs=[hbm] * 4,
        out_specs=hbm,
        scratch_shapes=[
            pltpu.SMEM(ctf_groups.shape, jnp.int32),
            pltpu.VMEM(ctf_table.shape, F32),
            pltpu.VMEM(images.shape, BF16),
            pltpu.VMEM(table.shape, BF16),
            pltpu.VMEM(images.shape, BF16),
            pltpu.VMEM(shape, BF16),
            pltpu.SemaphoreType.DMA((3 + table.shape[0],)),
            pltpu.SemaphoreType.DMA((table.shape[0],)),
        ],
        compiler_params=pltpu.CompilerParams(vmem_limit_bytes=60 * 2**20),
        name="transform",
    )(ctf_groups, ctf_table, images, table)
    parts, radial_basis, order_counts = lax.optimization_barrier((parts, radial_basis, order_counts))
    parts = lax.all_to_all(parts, ("img", "bas"), 0, 0, tiled=True, axis_index_groups=teams)
    orders = orders_dev // pool
    mine = lax.axis_index("img") % pool * orders
    counts = lax.dynamic_slice_in_dim(order_counts, mine, orders)
    basis = lax.dynamic_slice_in_dim(radial_basis, mine, orders)
    kept = jnp.arange(kmax, dtype=jnp.int32)[None, :] < counts[:, None]
    basis = jnp.where(kept[:, None, :], basis, jnp.zeros((), BF16))
    basis = basis.transpose(0, 2, 1).reshape(orders // 2, 2 * kmax, radii)
    rows = kmax // img_size
    pairs = orders // 2
    img_order = [n ^ (img_size // 64 * 42) for n in range(img_size)]
    sent = pl.pallas_call(
        functools.partial(covariances, place_of, img_order),
        out_shape=jax.ShapeDtypeStruct((kmax * pairs, 2 * kmax), F32),
        in_specs=[vmem, vmem],
        out_specs=vmem,
        scratch_shapes=[
            pltpu.VMEM(((pool * lows + 1) * lanes, radii), F32),
            pltpu.VMEM((kmax * pairs + 8, 2 * kmax), F32),
        ],
        compiler_params=pltpu.CompilerParams(vmem_limit_bytes=16 * 2**20),
        name="covariances",
    )(parts, basis)
    sent = sent.reshape(img_size, rows * pairs, 2 * kmax)
    got = lax.all_to_all(sent, "img", 0, 0, tiled=True, axis_index_groups=[img_order])
    gram = jnp.sum(got.reshape(img_size // pool, pool, rows, pairs, 2 * kmax), axis=0)
    gram = jnp.stack([gram[img_order[n] % pool] for n in range(pool)], axis=1)
    return gram.reshape(rows, orders_dev * kmax) * (1.0 / (images_dev * img_size))


def solution(mesh):
    placed = (P("img", "bas", None), P("img"), P(), P("bas", None, None), P("bas"))

    def step(polar_images, ctf_groups, ctf_table, radial_basis, order_counts):
        table = jnp.asarray(angular_table(radial_basis.shape[0], polar_images.shape[2]))
        return jax.shard_map(
            local, mesh=mesh, in_specs=(P(),) + placed, out_specs=P("img", "bas"), check_vma=False
        )(table, polar_images, ctf_groups, ctf_table, radial_basis, order_counts)

    return step
```

```python
import functools
import functools
import math

import jax
import jax.numpy as jnp
import ml_dtypes
import numpy as np
from jax import lax
from jax.experimental import pallas as pl
from jax.experimental.pallas import tpu as pltpu
from jax.sharding import PartitionSpec as P

F32, BF16 = jnp.float32, jnp.bfloat16
NT = (((1,), (1,)), ((), ()))


def angular_table(orders, angles):
    phase = np.arange(angles)[:, None] * np.arange(orders)[None, :] % angles
    theta = phase.astype(np.float32) * np.float32(2.0 * math.pi / angles)
    table = np.stack([np.cos(theta), np.sin(theta)], axis=-1) * np.float32(1.0 / math.sqrt(angles))
    table = table.reshape(angles // 8, 8, 2, orders).transpose(2, 0, 1, 3)
    return table.astype(ml_dtypes.bfloat16)


def transform(place_of, groups_in, ctf_in, images_in, table_in, parts_out, *scratch):
    groups, ctf, images, table, weighted, parts, sem_in, sem_out = scratch
    size, rows, lanes = parts.shape
    classes, radii = ctf.shape
    radii_dev = weighted.shape[0] // groups.shape[0]
    highs = weighted.shape[0] // rows
    width = lanes // highs
    halves = table.shape[0]
    copies = [
        pltpu.make_async_copy(source, target, sem_in.at[n])
        for n, (source, target) in enumerate(
            [(groups_in, groups), (ctf_in, ctf), (images_in, images)]
            + [(table_in.at[n], table.at[n]) for n in range(halves)]
        )
    ]
    for copy in copies:
        copy.start()
    first = lax.axis_index("bas") * radii_dev
    shape = (radii_dev, radii)
    own = lax.broadcasted_iota(jnp.int32, shape, 1) == first + lax.broadcasted_iota(jnp.int32, shape, 0)
    copies[0].wait()
    copies[1].wait()

    def weight(i):
        row = ctf[pl.ds(groups[i], 1), :]
        return jnp.sum(jnp.where(own, row, 0.0), axis=1, keepdims=True)

    step = 16 // radii_dev
    scales = [
        jnp.concatenate([weight(i + j) for j in range(step)], axis=0)
        for i in range(0, groups.shape[0], step)
    ]
    copies[2].wait()
    for n, scale in enumerate(scales):
        block = slice(n * 16, (n + 1) * 16)
        weighted[block, :] = (images[block, :].astype(F32) * scale).astype(BF16)
    group = lax.broadcasted_iota(jnp.int32, (rows, lanes), 1) // width
    for half in range(halves):
        copies[3 + half].wait()
    for half in range(halves):
        columns = table[half].reshape(weighted.shape[1], -1)
        spectra = jnp.dot(weighted[...], columns, preferred_element_type=F32)
        tiles = columns.shape[1] // lanes
        for tile in range(tiles):
            part = spectra[:, tile * lanes : (tile + 1) * lanes]
            blocks = [part[n * rows : (n + 1) * rows] for n in range(highs)]
            shift = highs // 2
            while shift:
                keep = (group & shift) == 0
                for n in range(highs):
                    if not n & shift:
                        one, two = blocks[n], blocks[n + shift]
                        turned_one = pltpu.roll(one, lanes - shift * width, 1)
                        turned_two = pltpu.roll(two, shift * width, 1)
                        blocks[n] = jnp.where(keep, one, turned_two)
                        blocks[n + shift] = jnp.where(keep, turned_one, two)
                shift //= 2
            for n, value in enumerate(blocks):
                place = place_of[(half * tiles + tile) * highs + n]
                parts[place] = value.astype(BF16)
    send = pltpu.make_async_copy(parts, parts_out, sem_out.at[0])
    send.start()
    send.wait()


def covariances(place_of, chunk_of, parts_ref, basis, out, by_order, staged):
    places, rows, lanes = parts_ref.shape
    pairs, wide, radii = basis.shape
    pool = len(place_of[0])
    sources = places // pool
    radii_dev = radii // sources
    lows = rows // radii_dev
    width = 4 * pairs
    highs = lanes // width
    half = wide // 2
    step = 16 // radii_dev
    blocks = pool * lows
    for i in range(0, lows, step):
        block = parts_ref[:, i * radii_dev : (i + step) * radii_dev, :].astype(F32)
        for j in range(step):
            for sub in range(pool):
                at = slice(j * radii_dev, (j + 1) * radii_dev)
                one = jnp.concatenate([block[place_of[n][sub]][at] for n in range(sources)], axis=0)
                n = (sub * lows + i + j) * lanes
                by_order[n : n + lanes, :] = one.T
    for pair in range(pairs):
        grams = []
        for order in range(2):
            rows_of = [
                by_order[pl.ds(high * width + 4 * pair + 2 * order + c, blocks, stride=lanes), :]
                for high in range(highs)
                for c in range(2)
            ]
            spectra = jnp.concatenate(rows_of, axis=0).astype(BF16)
            own = basis[pair, order * half : (order + 1) * half, :]
            coeffs = lax.dot_general(own, spectra, NT, preferred_element_type=F32).astype(BF16)
            grams.append(lax.dot_general(coeffs, coeffs, NT, preferred_element_type=F32))
        staged[pl.ds(pair, half, stride=pairs), :] = jnp.concatenate(grams, axis=1)
    count = len(chunk_of) // 2
    step = out.shape[0] // count
    for here in range(count):
        there = chunk_of[2 * here] // 2
        out[here * step : (here + 1) * step, :] = staged[there * step : (there + 1) * step, :]


def local(table, polar_images, ctf_groups, ctf_table, radial_basis, order_counts):
    images_dev, radii_dev, angles = polar_images.shape
    orders_dev, radii, kmax = radial_basis.shape
    img_size, bas_size = lax.axis_size("img"), lax.axis_size("bas")
    hbm = pl.BlockSpec(memory_space=pltpu.HBM)
    vmem = pl.BlockSpec(memory_space=pltpu.VMEM)
    pool = 4
    lanes = 128
    lows = images_dev * orders_dev * 2 // pool // lanes
    places = bas_size * pool
    shape = (places, lows * radii_dev, lanes)
    ring = [(high, sub, core) for high in range(bas_size // 2) for sub in range(pool) for core in range(2)]
    start = 5 * places // 8
    ring = ring[start:] + ring[:start]
    members = [(sub, 2 * high + core) for high, sub, core in ring]
    place_of = [[members.index((sub, bas)) for sub in range(pool)] for bas in range(bas_size)]
    teams = [
        [(team * pool + sub) * bas_size + bas for sub, bas in members] for team in range(img_size // pool)
    ]
    images = polar_images.reshape(-1, angles)
    parts = pl.pallas_call(
        functools.partial(transform, sum(place_of, [])),
        out_shape=jax.ShapeDtypeStruct(shape, BF16),
        in_specs=[hbm] * 4,
        out_specs=hbm,
        scratch_shapes=[
            pltpu.SMEM(ctf_groups.shape, jnp.int32),
            pltpu.VMEM(ctf_table.shape, F32),
            pltpu.VMEM(images.shape, BF16),
            pltpu.VMEM(table.shape, BF16),
            pltpu.VMEM(images.shape, BF16),
            pltpu.VMEM(shape, BF16),
            pltpu.SemaphoreType.DMA((3 + table.shape[0],)),
            pltpu.SemaphoreType.DMA((1,)),
        ],
        compiler_params=pltpu.CompilerParams(vmem_limit_bytes=60 * 2**20),
        name="transform",
    )(ctf_groups, ctf_table, images, table)
    parts, radial_basis, order_counts = lax.optimization_barrier((parts, radial_basis, order_counts))
    parts = lax.all_to_all(parts, ("img", "bas"), 0, 0, tiled=True, axis_index_groups=teams)
    orders = orders_dev // pool
    mine = lax.axis_index("img") % pool * orders
    counts = lax.dynamic_slice_in_dim(order_counts, mine, orders)
    basis = lax.dynamic_slice_in_dim(radial_basis, mine, orders)
    kept = jnp.arange(kmax, dtype=jnp.int32)[None, :] < counts[:, None]
    basis = jnp.where(kept[:, None, :], basis, jnp.zeros((), BF16))
    basis = basis.transpose(0, 2, 1).reshape(orders // 2, 2 * kmax, radii)
    rows = kmax // img_size
    pairs = orders // 2
    img_order = [n ^ (img_size // 64 * 42) for n in range(img_size)]
    sent = pl.pallas_call(
        functools.partial(covariances, place_of, img_order),
        out_shape=jax.ShapeDtypeStruct((kmax * pairs, 2 * kmax), F32),
        in_specs=[vmem, vmem],
        out_specs=vmem,
        scratch_shapes=[
            pltpu.VMEM(((pool * lows + 1) * lanes, radii), F32),
            pltpu.VMEM((kmax * pairs + 8, 2 * kmax), F32),
        ],
        compiler_params=pltpu.CompilerParams(vmem_limit_bytes=16 * 2**20),
        name="covariances",
    )(parts, basis)
    sent = sent.reshape(img_size, rows * pairs, 2 * kmax)
    got = lax.all_to_all(sent, "img", 0, 0, tiled=True, axis_index_groups=[img_order])
    gram = jnp.sum(got.reshape(img_size // pool, pool, rows, pairs, 2 * kmax), axis=0)
    gram = jnp.stack([gram[img_order[n] % pool] for n in range(pool)], axis=1)
    return gram.reshape(rows, orders_dev * kmax) * (1.0 / (images_dev * img_size))


def solution(mesh):
    placed = (P("img", "bas", None), P("img"), P(), P("bas", None, None), P("bas"))

    def step(polar_images, ctf_groups, ctf_table, radial_basis, order_counts):
        table = jnp.asarray(angular_table(radial_basis.shape[0], polar_images.shape[2]))
        return jax.shard_map(
            local, mesh=mesh, in_specs=(P(),) + placed, out_specs=P("img", "bas"), check_vma=False
        )(table, polar_images, ctf_groups, ctf_table, radial_basis, order_counts)

    return step
```

```python
import functools
import functools
import math

import jax
import jax.numpy as jnp
import ml_dtypes
import numpy as np
from jax import lax
from jax.experimental import pallas as pl
from jax.experimental.pallas import tpu as pltpu
from jax.sharding import PartitionSpec as P

F32, BF16 = jnp.float32, jnp.bfloat16
NT = (((1,), (1,)), ((), ()))


def angular_table(orders, angles):
    phase = np.arange(angles)[:, None] * np.arange(orders)[None, :] % angles
    theta = phase.astype(np.float32) * np.float32(2.0 * math.pi / angles)
    table = np.stack([np.cos(theta), np.sin(theta)], axis=-1) * np.float32(1.0 / math.sqrt(angles))
    table = table.reshape(angles // 8, 8, 2, orders).transpose(2, 0, 1, 3)
    return table.astype(ml_dtypes.bfloat16)


def transform(place_of, groups_in, ctf_in, images_in, table_in, parts_out, *scratch):
    groups, ctf, images, table, weighted, parts, sem_in, sem_out = scratch
    size, rows, lanes = parts.shape
    classes, radii = ctf.shape
    radii_dev = weighted.shape[0] // groups.shape[0]
    highs = weighted.shape[0] // rows
    width = lanes // highs
    halves = table.shape[0]
    copies = [
        pltpu.make_async_copy(source, target, sem_in.at[n])
        for n, (source, target) in enumerate(
            [(groups_in, groups), (ctf_in, ctf), (images_in, images)]
            + [(table_in.at[n], table.at[n]) for n in range(halves)]
        )
    ]
    for copy in copies:
        copy.start()
    first = lax.axis_index("bas") * radii_dev
    shape = (radii_dev, radii)
    own = lax.broadcasted_iota(jnp.int32, shape, 1) == first + lax.broadcasted_iota(jnp.int32, shape, 0)
    copies[0].wait()
    copies[1].wait()

    def weight(i):
        row = ctf[pl.ds(groups[i], 1), :]
        return jnp.sum(jnp.where(own, row, 0.0), axis=1, keepdims=True)

    step = 16 // radii_dev
    scales = [
        jnp.concatenate([weight(i + j) for j in range(step)], axis=0)
        for i in range(0, groups.shape[0], step)
    ]
    copies[2].wait()
    for n, scale in enumerate(scales):
        block = slice(n * 16, (n + 1) * 16)
        weighted[block, :] = (images[block, :].astype(F32) * scale).astype(BF16)
    group = lax.broadcasted_iota(jnp.int32, (rows, lanes), 1) // width
    for half in range(halves):
        copies[3 + half].wait()
    for half in range(halves):
        columns = table[half].reshape(weighted.shape[1], -1)
        spectra = jnp.dot(weighted[...], columns, preferred_element_type=F32)
        tiles = columns.shape[1] // lanes
        for tile in range(tiles):
            part = spectra[:, tile * lanes : (tile + 1) * lanes]
            blocks = [part[n * rows : (n + 1) * rows] for n in range(highs)]
            shift = highs // 2
            while shift:
                keep = (group & shift) == 0
                for n in range(highs):
                    if not n & shift:
                        one, two = blocks[n], blocks[n + shift]
                        turned_one = pltpu.roll(one, lanes - shift * width, 1)
                        turned_two = pltpu.roll(two, shift * width, 1)
                        blocks[n] = jnp.where(keep, one, turned_two)
                        blocks[n + shift] = jnp.where(keep, turned_one, two)
                shift //= 2
            for n, value in enumerate(blocks):
                place = place_of[(half * tiles + tile) * highs + n]
                parts[place] = value.astype(BF16)
    send = pltpu.make_async_copy(parts, parts_out, sem_out.at[0])
    send.start()
    send.wait()


def covariances(place_of, chunk_of, parts_ref, basis, out, by_order, staged):
    places, rows, lanes = parts_ref.shape
    pairs, wide, radii = basis.shape
    pool = len(place_of[0])
    sources = places // pool
    radii_dev = radii // sources
    lows = rows // radii_dev
    width = 4 * pairs
    highs = lanes // width
    half = wide // 2
    step = 16 // radii_dev
    blocks = pool * lows
    for i in range(0, lows, step):
        block = parts_ref[:, i * radii_dev : (i + step) * radii_dev, :].astype(F32)
        for j in range(step):
            for sub in range(pool):
                at = slice(j * radii_dev, (j + 1) * radii_dev)
                one = jnp.concatenate([block[place_of[n][sub]][at] for n in range(sources)], axis=0)
                n = (sub * lows + i + j) * lanes
                by_order[n : n + lanes, :] = one.T
    samples = 2 * highs * blocks
    shape = (wide, 2 * samples)
    same = (lax.broadcasted_iota(jnp.int32, shape, 0) < half) == (
        lax.broadcasted_iota(jnp.int32, shape, 1) < samples
    )
    for pair in range(pairs):
        rows_of = [
            by_order[pl.ds(high * width + 4 * pair + 2 * order + c, blocks, stride=lanes), :]
            for order in range(2)
            for high in range(highs)
            for c in range(2)
        ]
        spectra = jnp.concatenate(rows_of, axis=0).astype(BF16)
        coeffs = lax.dot_general(basis[pair], spectra, NT, preferred_element_type=F32)
        coeffs = jnp.where(same, coeffs, 0.0).astype(BF16)
        gram = lax.dot_general(coeffs, coeffs, NT, preferred_element_type=F32)
        staged[pl.ds(pair, half, stride=pairs), :] = gram[:half] + gram[half:]
    count = len(chunk_of) // 2
    step = out.shape[0] // count
    for here in range(count):
        there = chunk_of[2 * here] // 2
        out[here * step : (here + 1) * step, :] = staged[there * step : (there + 1) * step, :]


def local(table, polar_images, ctf_groups, ctf_table, radial_basis, order_counts):
    images_dev, radii_dev, angles = polar_images.shape
    orders_dev, radii, kmax = radial_basis.shape
    img_size, bas_size = lax.axis_size("img"), lax.axis_size("bas")
    hbm = pl.BlockSpec(memory_space=pltpu.HBM)
    vmem = pl.BlockSpec(memory_space=pltpu.VMEM)
    pool = 4
    lanes = 128
    lows = images_dev * orders_dev * 2 // pool // lanes
    places = bas_size * pool
    shape = (places, lows * radii_dev, lanes)
    ring = [(high, sub, core) for high in range(bas_size // 2) for sub in range(pool) for core in range(2)]
    start = 11 * places // 16
    ring = ring[start:] + ring[:start]
    members = [(sub, 2 * high + core) for high, sub, core in ring]
    place_of = [[members.index((sub, bas)) for sub in range(pool)] for bas in range(bas_size)]
    teams = [
        [(team * pool + sub) * bas_size + bas for sub, bas in members] for team in range(img_size // pool)
    ]
    images = polar_images.reshape(-1, angles)
    parts = pl.pallas_call(
        functools.partial(transform, sum(place_of, [])),
        out_shape=jax.ShapeDtypeStruct(shape, BF16),
        in_specs=[hbm] * 4,
        out_specs=hbm,
        scratch_shapes=[
            pltpu.SMEM(ctf_groups.shape, jnp.int32),
            pltpu.VMEM(ctf_table.shape, F32),
            pltpu.VMEM(images.shape, BF16),
            pltpu.VMEM(table.shape, BF16),
            pltpu.VMEM(images.shape, BF16),
            pltpu.VMEM(shape, BF16),
            pltpu.SemaphoreType.DMA((3 + table.shape[0],)),
            pltpu.SemaphoreType.DMA((1,)),
        ],
        compiler_params=pltpu.CompilerParams(vmem_limit_bytes=60 * 2**20),
        name="transform",
    )(ctf_groups, ctf_table, images, table)
    parts, radial_basis, order_counts = lax.optimization_barrier((parts, radial_basis, order_counts))
    parts = lax.all_to_all(parts, ("img", "bas"), 0, 0, tiled=True, axis_index_groups=teams)
    orders = orders_dev // pool
    mine = lax.axis_index("img") % pool * orders
    counts = lax.dynamic_slice_in_dim(order_counts, mine, orders)
    basis = lax.dynamic_slice_in_dim(radial_basis, mine, orders)
    kept = jnp.arange(kmax, dtype=jnp.int32)[None, :] < counts[:, None]
    basis = jnp.where(kept[:, None, :], basis, jnp.zeros((), BF16))
    basis = basis.transpose(0, 2, 1).reshape(orders // 2, 2 * kmax, radii)
    rows = kmax // img_size
    pairs = orders // 2
    img_order = [n ^ (img_size // 64 * 42) for n in range(img_size)]
    sent = pl.pallas_call(
        functools.partial(covariances, place_of, img_order),
        out_shape=jax.ShapeDtypeStruct((kmax * pairs, 2 * kmax), F32),
        in_specs=[vmem, vmem],
        out_specs=vmem,
        scratch_shapes=[
            pltpu.VMEM(((pool * lows + 1) * lanes, radii), F32),
            pltpu.VMEM((kmax * pairs + 8, 2 * kmax), F32),
        ],
        compiler_params=pltpu.CompilerParams(vmem_limit_bytes=16 * 2**20),
        name="covariances",
    )(parts, basis)
    sent = sent.reshape(img_size, rows * pairs, 2 * kmax)
    got = lax.all_to_all(sent, "img", 0, 0, tiled=True, axis_index_groups=[img_order])
    gram = jnp.sum(got.reshape(img_size // pool, pool, rows, pairs, 2 * kmax), axis=0)
    gram = jnp.stack([gram[img_order[n] % pool] for n in range(pool)], axis=1)
    return gram.reshape(rows, orders_dev * kmax) * (1.0 / (images_dev * img_size))


def solution(mesh):
    placed = (P("img", "bas", None), P("img"), P(), P("bas", None, None), P("bas"))

    def step(polar_images, ctf_groups, ctf_table, radial_basis, order_counts):
        table = jnp.asarray(angular_table(radial_basis.shape[0], polar_images.shape[2]))
        return jax.shard_map(
            local, mesh=mesh, in_specs=(P(),) + placed, out_specs=P("img", "bas"), check_vma=False
        )(table, polar_images, ctf_groups, ctf_table, radial_basis, order_counts)

    return step
```
